128 devices in a mesh: chan: 32 (over z, y, core), win: 4 (over x).
Axes of the slice: x: 4, y: 4, z: 4, core: 2. Of those that a mesh axis runs over, the one named last changes fastest.
Arguments:
- spectra: float32 [8, 2, 512, 4096], P('win', None, 'chan'), may hold values from -500 to 500, as said below
- plan: int32 [4], replicated, may hold values from 0 to 31, as said below
- pair_bins: int32 [512, 64, 1], P('chan'), may hold values from 0 to 255; in each aligned block of 1024 rows (0 to 1023, 1024 to 2047, ..., all dimensions but the last counted through in order) at most 8 rows name the same one
Outputs:
- stack: float32 [256, 512], P('chan')
The draws below stay inside these ranges and needn't reach their ends.
Inputs may be any that keep to these rules, and one draw needn't show every extreme that they name: Float spectra with channel and bin scales of order one to ten. `plan`: 4 distinct block indices. `pair_bins`: among the pairs of one device's receivers (16 channels, aligned blocks of rows), no bin is named more than 8 times, a bound that some block reaches. Every bin is named by some pair.
All inputs are finite; a program needn't handle non-finite values.
Results may differ from the reference program's by a relative error of at most 0.0051.
Values may be sent and summed in bfloat16 or wider, within the bound.
No kernel may reach another device: no remote copies, remote signals or barrier semaphores. Data moves between devices by JAX's collectives and lax.ppermute only.
A program may use at most 64 MiB of HBM per device.

```python
import math
import jax
import jax.numpy as jnp
import numpy as np
from jax import lax

CH_DEV = 16
FREQ = 4096
LAGS = 512
BAND = 128
STEPS = 4
NBINS = 256
CAP = 8
CHANNELS = 512
WINDOWS = 8
N_CHAN = 32


def draw_spectra(key, part):
    key = jax.random.fold_in(key, 7)
    subkeys = jax.random.split(key, 3)
    full_shape = (WINDOWS, 2, CHANNELS, FREQ)
    samples = jnp.clip(jax.random.normal(subkeys[0], full_shape, jnp.float32), -5.0, 5.0)
    spread = math.log(10.0)
    channel_scale = jnp.exp(spread * jax.random.uniform(subkeys[1], (1, 1, CHANNELS, 1), jnp.float32))
    bin_scale = jnp.exp(spread * jax.random.uniform(subkeys[2], (WINDOWS, 1, 1, FREQ), jnp.float32))
    return samples * channel_scale * bin_scale


def draw_plan(key, part):
    key = jax.random.fold_in(key, 11)
    order_key, pick_key = jax.random.split(key)
    middle = 1 + jax.random.permutation(pick_key, N_CHAN - 2)[:STEPS - 2]
    chosen = jnp.concatenate([jnp.array([0, N_CHAN - 1], jnp.int32), middle.astype(jnp.int32)])
    return jax.random.permutation(order_key, chosen).astype(jnp.int32)


def assign_block(key, own, number, rows, number_of, top, bound, lean):
    sequence = jax.random.permutation(key, number_of)
    packed, usual = load_shares(number_of, rows * top, bound, lean, True), load_shares(number_of, rows * top, bound, lean, False)
    places = jnp.arange(number_of)

    def named(sizes, offset_by):
        used = int((sizes > 0).sum())
        fixed = max(1, used // 4)
        moved = fixed + (places - fixed + offset_by * (used - fixed)) % max(1, number_of - fixed)
        return jnp.zeros((number_of,), jnp.int32).at[sequence[jnp.where(places < fixed, places, moved)]].set(jnp.asarray(sizes, jnp.int32))

    sizes = jnp.where(number % 4 == 0, named(packed, number // 4), named(usual, number - number // 4 - 1))
    mixed = jax.random.permutation(jax.random.fold_in(own, 3), number_of)
    donor, sink = mixed[0:number_of // 2 * 2:2], mixed[1:number_of // 2 * 2:2]
    slack = jnp.minimum(sizes[donor] - 1, bound - sizes[sink]) // 2
    slack = jnp.where((donor == sequence[0]) | (sink == sequence[0]) | (sizes[sink] == 0), 0, jnp.maximum(slack, 0))
    moved = jax.random.randint(jax.random.fold_in(own, 4), (number_of // 2,), 0, 1 << 20) % (slack + 1)
    sizes = sizes.at[donor].add(-moved).at[sink].add(moved)
    items = jnp.searchsorted(jnp.cumsum(sizes), jnp.arange(rows * top), side="right").astype(jnp.int32)
    listing = items.reshape(top, rows).T
    listing = listing[jax.random.permutation(jax.random.fold_in(own, 1), rows)]
    offset_by = jax.random.randint(jax.random.fold_in(own, 2), (rows, 1), 0, top)
    return jnp.take_along_axis(listing, (jnp.arange(top)[None, :] + offset_by) % top, axis=1)


def load_shares(amount, total, most, skew, full):
    weights = [(1 << 20) // math.isqrt(standing ** skew) + 1 for standing in range(1, amount + 1)]
    largest = most if full else min(most, max(-(-total // amount), total * weights[0] // sum(weights)))
    least = 1 if total - largest >= amount - 1 else 0
    holding, rest = [largest] + [least] * (amount - 1), total - largest - least * (amount - 1)
    while rest > 0:
        movable = [i for i in range(1, amount) if holding[i] < largest] or [i for i in range(1, amount) if holding[i] < most]
        mass, remaining = sum([weights[i] for i in movable]), rest
        for i in movable:
            more = min(most - holding[i], max(1, remaining * weights[i] // mass), rest)
            holding[i] = holding[i] + more
            rest = rest - more
    return np.array(holding)


def setup_inputs(seed: int = 0) -> dict:
    splits = jax.random.split(jax.random.key(seed), 4)
    spectra = draw_spectra(jax.random.fold_in(splits[3], 71), 0)
    plan = draw_plan(jax.random.fold_in(splits[3], 71), 0)
    pair_bins_keys = jax.random.split(jax.random.fold_in(splits[2], 1), CHANNELS * (STEPS * CH_DEV) // (CH_DEV * STEPS * CH_DEV))
    pair_bins_turns = jax.random.permutation(jax.random.fold_in(splits[2], 3), CHANNELS * (STEPS * CH_DEV) // (CH_DEV * STEPS * CH_DEV))
    pair_bins = jax.vmap(lambda own, number: assign_block(jax.random.fold_in(splits[2], 2), own, number, CH_DEV * STEPS * CH_DEV, NBINS, 1, CAP, 2))(pair_bins_keys, pair_bins_turns).reshape((CHANNELS, STEPS * CH_DEV, 1))
    return {"spectra": spectra, "plan": plan, "pair_bins": pair_bins}


def whiten(spectra):
    energy = spectra[:, 0] ** 2 + spectra[:, 1] ** 2
    banded = energy.reshape(energy.shape[0], energy.shape[1], -1, BAND)
    band_level = jnp.sqrt(lax.optimization_barrier(jnp.mean(banded, axis=3)) + 1e-06)
    level_full = jnp.repeat(band_level, BAND, axis=2)
    return (spectra / level_full[:, None]).astype(jnp.bfloat16)

def lag_table(offset, span_bins, lag_count, bin_total):
    numbers = offset + 1 + lax.iota(jnp.int32, span_bins)
    shifts = lax.iota(jnp.int32, lag_count) - lag_count // 2
    phase = jnp.mod(numbers[:, None] * shifts[None, :], 2 * bin_total)
    angle = phase.astype(jnp.float32) * (math.pi / bin_total)
    factor = 1.0 / math.sqrt(bin_total)
    return (jnp.stack([jnp.cos(angle), -jnp.sin(angle)]) * factor).astype(jnp.bfloat16)

def cross_rows(source, receiver):
    source_real = jnp.transpose(source[:, 0].astype(jnp.float32), (1, 0, 2))[None]
    source_imaginary = jnp.transpose(source[:, 1].astype(jnp.float32), (1, 0, 2))[None]
    receiver_real = jnp.transpose(receiver[:, 0].astype(jnp.float32), (1, 0, 2))[:, None]
    receiver_imaginary = jnp.transpose(receiver[:, 1].astype(jnp.float32), (1, 0, 2))[:, None]
    product_real = source_real * receiver_real + source_imaginary * receiver_imaginary
    product_imaginary = source_imaginary * receiver_real - source_real * receiver_imaginary
    joined = jnp.stack([product_real, product_imaginary], axis=3).astype(jnp.bfloat16)
    return joined.reshape(joined.shape[0] * joined.shape[1], -1)

def reference(spectra, plan, pair_bins):
    whitened = whiten(spectra)
    window_count = spectra.shape[0]
    table_block = lag_table(0, FREQ, LAGS, FREQ)
    table_full = jnp.broadcast_to(table_block[None], (window_count,) + table_block.shape).reshape(window_count * 2 * FREQ, LAGS)
    blocks = jnp.moveaxis(whitened.reshape(window_count, 2, N_CHAN, CH_DEV, FREQ), 2, 0)
    per_step = []
    for source_step in range(STEPS):
        first_channel = (plan[source_step] * CH_DEV).astype(jnp.int32)
        source = lax.dynamic_slice_in_dim(whitened, first_channel, CH_DEV, 2)

        def correlate(receiver):
            result = jnp.dot(cross_rows(source, receiver), table_full, preferred_element_type=jnp.float32)
            return result.reshape(CH_DEV, CH_DEV, LAGS)
        traces_step = lax.map(correlate, blocks)
        per_step.append(traces_step.reshape(N_CHAN * CH_DEV, CH_DEV, LAGS))
    traces = jnp.stack(per_step, axis=1).reshape(-1, LAGS)
    segment_ids = pair_bins.reshape(-1).astype(jnp.int32)
    bin_sums = jax.ops.segment_sum(traces, segment_ids, num_segments=NBINS)
    counts = jax.ops.segment_sum(jnp.ones(segment_ids.shape, jnp.float32), segment_ids, num_segments=NBINS)
    return bin_sums / jnp.sqrt(counts * WINDOWS)[:, None]
```

```python
import functools
import math

import jax
import jax.numpy as jnp
from jax import lax
from jax.experimental import pallas as pl
from jax.experimental.pallas import tpu as pltpu
from jax.sharding import PartitionSpec as P

LAGS = 512
BAND = 128
STEPS = 4
NBINS = 256
CH = 16
SOURCES = STEPS * CH
JBLK = 4


def whiten_kernel(spectra_ref, bins_ref, out_ref):
    chunks = out_ref.shape[0]
    windows = spectra_ref.shape[0]
    bins = bins_ref[...].astype(jnp.float32)
    bins = jnp.concatenate([bins, jnp.zeros_like(bins)], axis=1).astype(jnp.bfloat16)
    for c in range(chunks):
        lanes = pl.ds(c * BAND, BAND)
        for w in range(windows):
            real = spectra_ref[w, 0, :, lanes]
            imaginary = spectra_ref[w, 1, :, lanes]
            energy = real * real + imaginary * imaginary
            level = jnp.sqrt(jnp.mean(energy, axis=1, keepdims=True) + 1e-06)
            out_ref[c, pl.ds(2 * w * CH, CH), :] = (real / level).astype(jnp.bfloat16)
            out_ref[c, pl.ds((2 * w + 1) * CH, CH), :] = (imaginary / level).astype(jnp.bfloat16)
        out_ref[c, pl.ds(2 * windows * CH, CH), :] = bins


def whiten(spectra, bins):
    windows, _, channels, freq = spectra.shape
    owners = freq // BAND
    rows = 2 * windows * CH + CH
    step = 4
    return pl.pallas_call(
        whiten_kernel,
        grid=(owners // step,),
        in_specs=[
            pl.BlockSpec((windows, 2, channels, step * BAND), lambda i: (0, 0, 0, i)),
            pl.BlockSpec(bins.shape, lambda i: (0, 0)),
        ],
        out_specs=pl.BlockSpec((step, rows, BAND), lambda i: (i, 0, 0)),
        out_shape=jax.ShapeDtypeStruct((owners, rows, BAND), jnp.bfloat16),
    )(spectra, bins)


def bin_kernel(windows, plan_ref, x_ref, table_ref, out_ref, rec_ref, src_ref, bt_ref, sums_ref):
    owners = x_ref.shape[0]
    channels = owners * CH
    parts = 2 * windows
    for p in range(parts):
        rec_ref[p] = x_ref[:, pl.ds(p * CH, CH), :].reshape(channels, BAND)
    for q in range(STEPS):
        for p in range(parts):
            slab = x_ref[plan_ref[q], pl.ds(p * CH, CH), :].astype(jnp.float32)
            for j in range(CH):
                row = jnp.broadcast_to(slab[j:j + 1, :], (CH, BAND))
                src_ref[q * CH + j, p] = row.astype(jnp.bfloat16)
    bins = x_ref[:, pl.ds(parts * CH, CH), :].reshape(channels, BAND).astype(jnp.float32)
    turned = bins.T
    for j in range(SOURCES):
        row = jnp.broadcast_to(turned[j:j + 1, :], (CH, channels))
        bt_ref[j] = row.astype(jnp.bfloat16)
    sums_ref[...] = jnp.zeros_like(sums_ref)

    def step(index, carry):
        numbers = lax.broadcasted_iota(jnp.int32, (NBINS, channels), 0).astype(jnp.float32)
        numbers = numbers.astype(jnp.bfloat16)
        one = jnp.ones((), jnp.bfloat16)
        zero = jnp.zeros((), jnp.bfloat16)
        hots = []
        crosses = []
        for k in range(JBLK):
            j = index * JBLK + k
            named = jnp.broadcast_to(bt_ref[j][None], (NBINS // CH, CH, channels))
            hots.append(jnp.where(numbers == named.reshape(NBINS, channels), one, zero))
            total_real = None
            for w in range(windows):
                sr = src_ref[j, 2 * w][None]
                si = src_ref[j, 2 * w + 1][None]
                rr = rec_ref[2 * w].reshape(owners, CH, BAND)
                ri = rec_ref[2 * w + 1].reshape(owners, CH, BAND)
                real = sr * rr + si * ri
                imaginary = si * rr - sr * ri
                if total_real is None:
                    total_real, total_imaginary = real, imaginary
                else:
                    total_real = total_real + real
                    total_imaginary = total_imaginary + imaginary
            crosses.append(
                jnp.concatenate([total_real, total_imaginary], axis=2).reshape(channels, 2 * BAND)
            )
        hot = jnp.concatenate(hots, axis=1)
        cross = jnp.concatenate(crosses, axis=0)
        sums_ref[...] += jnp.dot(hot, cross, preferred_element_type=jnp.float32)
        return carry

    lax.fori_loop(0, SOURCES // JBLK, step, 0)
    sums = sums_ref[...]
    high = sums.astype(jnp.bfloat16)
    low = (sums - high.astype(jnp.float32)).astype(jnp.bfloat16)
    table = table_ref[...]
    lags = jnp.dot(high, table, preferred_element_type=jnp.float32)
    lags = lags + jnp.dot(low, table, preferred_element_type=jnp.float32)
    out_ref[...] = lags.astype(jnp.bfloat16)


def bin_sums(plan, gathered, table, windows):
    owners, rows, _ = gathered.shape
    channels = owners * CH
    vmem = pl.BlockSpec(memory_space=pltpu.VMEM)
    return pl.pallas_call(
        functools.partial(bin_kernel, windows),
        in_specs=[pl.BlockSpec(memory_space=pltpu.SMEM), vmem, vmem],
        out_specs=vmem,
        out_shape=jax.ShapeDtypeStruct((NBINS, LAGS), jnp.bfloat16),
        scratch_shapes=[
            pltpu.VMEM((2 * windows, channels, BAND), jnp.bfloat16),
            pltpu.VMEM((SOURCES, 2 * windows, CH, BAND), jnp.bfloat16),
            pltpu.VMEM((SOURCES, CH, channels), jnp.bfloat16),
            pltpu.VMEM((NBINS, 2 * BAND), jnp.float32),
        ],
        compiler_params=pltpu.CompilerParams(vmem_limit_bytes=40 * 1024 * 1024),
    )(plan, gathered, table)


def lag_table(offset, span_bins, lag_count, bin_total):
    numbers = offset + 1 + lax.iota(jnp.int32, span_bins)
    shifts = lax.iota(jnp.int32, lag_count) - lag_count // 2
    phase = jnp.mod(numbers[:, None] * shifts[None, :], 2 * bin_total)
    angle = phase.astype(jnp.float32) * (math.pi / bin_total)
    factor = 1.0 / math.sqrt(bin_total)
    table = (jnp.stack([jnp.cos(angle), -jnp.sin(angle)]) * factor).astype(jnp.bfloat16)
    return table.reshape(2 * span_bins, lag_count)


def per_device(spectra, plan, pair_bins):
    windows = spectra.shape[0]
    freq = spectra.shape[3]
    owners = lax.axis_size("chan")
    win_size = lax.axis_size("win")
    own = lax.axis_index("chan")
    outgoing = whiten(spectra, pair_bins.reshape(CH, SOURCES))
    gathered = lax.all_to_all(outgoing, "chan", split_axis=0, concat_axis=0, tiled=True)
    table = lag_table(own * BAND, BAND, LAGS, freq)
    partial = bin_sums(plan, gathered, table, windows)
    bin_block = NBINS // owners
    arrived = lax.all_to_all(
        partial.reshape(owners, bin_block, LAGS), "chan", split_axis=0, concat_axis=0, tiled=True
    )
    total = jnp.sum(arrived.astype(jnp.float32), axis=0)
    named = gathered[:, 2 * windows * CH:, :SOURCES].astype(jnp.float32)
    mine = (own * bin_block + lax.iota(jnp.int32, bin_block)).astype(jnp.float32)
    counts = jnp.sum((named[None] == mine[:, None, None, None]).astype(jnp.float32), axis=(1, 2, 3))
    summed = total
    for d in range(1, win_size):
        summed = summed + lax.ppermute(
            total, "win", [(i, (i + d) % win_size) for i in range(win_size)]
        )
    return summed / jnp.sqrt(counts * (windows * win_size))[:, None]


def solution(mesh):
    placed = (P("win", None, "chan", None), P(), P("chan", None, None))
    return jax.shard_map(
        per_device, mesh=mesh, in_specs=placed, out_specs=P("chan", None), check_vma=False
    )
```

```python
import functools
import math

import jax
import jax.numpy as jnp
from jax import lax
from jax.experimental import pallas as pl
from jax.experimental.pallas import tpu as pltpu
from jax.sharding import PartitionSpec as P

LAGS = 512
BAND = 128
STEPS = 4
NBINS = 256
CH = 16
SOURCES = STEPS * CH
JBLK = 16


def whiten_kernel(spectra_ref, bins_ref, out_ref):
    chunks = out_ref.shape[0]
    windows = spectra_ref.shape[0]
    bins = bins_ref[...].astype(jnp.float32)
    bins = jnp.concatenate([bins, jnp.zeros_like(bins)], axis=1).astype(jnp.bfloat16)
    for c in range(chunks):
        lanes = pl.ds(c * BAND, BAND)
        for w in range(windows):
            real = spectra_ref[w, 0, :, lanes]
            imaginary = spectra_ref[w, 1, :, lanes]
            energy = real * real + imaginary * imaginary
            level = jnp.sqrt(jnp.mean(energy, axis=1, keepdims=True) + 1e-06)
            inverse = 1.0 / level
            out_ref[c, pl.ds(2 * w * CH, CH), :] = (real * inverse).astype(jnp.bfloat16)
            out_ref[c, pl.ds((2 * w + 1) * CH, CH), :] = (imaginary * inverse).astype(jnp.bfloat16)
        out_ref[c, pl.ds(2 * windows * CH, CH), :] = bins


def whiten(spectra, bins):
    windows, _, channels, freq = spectra.shape
    owners = freq // BAND
    rows = 2 * windows * CH + CH
    step = 16
    return pl.pallas_call(
        whiten_kernel,
        grid=(owners // step,),
        in_specs=[
            pl.BlockSpec((windows, 2, channels, step * BAND), lambda i: (0, 0, 0, i)),
            pl.BlockSpec(bins.shape, lambda i: (0, 0)),
        ],
        out_specs=pl.BlockSpec((step, rows, BAND), lambda i: (i, 0, 0)),
        out_shape=jax.ShapeDtypeStruct((owners, rows, BAND), jnp.bfloat16),
    )(spectra, bins)


def hot_rows(bt_ref, j, channels):
    numbers = lax.broadcasted_iota(jnp.int32, (NBINS, channels), 0).astype(jnp.float32)
    named = jnp.broadcast_to(bt_ref[j][None], (NBINS // CH, CH, channels))
    same = numbers.astype(jnp.bfloat16) == named.reshape(NBINS, channels)
    return jnp.where(same, jnp.ones((), jnp.bfloat16), jnp.zeros((), jnp.bfloat16))


def cross_piece(source, receiver, windows):
    first = second = third = None
    for w in range(windows):
        products = [source[3 * w + p] * receiver[3 * w + p] for p in range(3)]
        if first is None:
            first, second, third = products
        else:
            first = first + products[0]
            second = second + products[1]
            third = third + products[2]
    real = (first - third).astype(jnp.bfloat16)
    imaginary = (first + second).astype(jnp.bfloat16)
    return jnp.concatenate([real, imaginary], axis=1)


def bin_kernel(windows, plan_ref, x_ref, table_ref, out_ref, rec_ref, src_ref, bt_ref, sums_ref):
    owners = x_ref.shape[0]
    channels = owners * CH
    for w in range(windows):
        real = x_ref[:, pl.ds(2 * w * CH, CH), :].reshape(channels, BAND).astype(jnp.float32)
        imaginary = x_ref[:, pl.ds((2 * w + 1) * CH, CH), :].reshape(channels, BAND)
        imaginary = imaginary.astype(jnp.float32)
        rec_ref[3 * w] = real
        rec_ref[3 * w + 1] = -(real + imaginary)
        rec_ref[3 * w + 2] = real - imaginary
    for q in range(STEPS):
        for w in range(windows):
            real = x_ref[plan_ref[q], pl.ds(2 * w * CH, CH), :].astype(jnp.float32)
            imaginary = x_ref[plan_ref[q], pl.ds((2 * w + 1) * CH, CH), :].astype(jnp.float32)
            for p, value in enumerate((real + imaginary, real, imaginary)):
                for j in range(CH):
                    row = jnp.broadcast_to(value[j:j + 1, :], (8, BAND))
                    src_ref[q * CH + j, 3 * w + p] = row
    bins = x_ref[:, pl.ds(2 * windows * CH, CH), :].reshape(channels, BAND).astype(jnp.float32)
    turned = bins.T
    for j in range(SOURCES):
        row = jnp.broadcast_to(turned[j:j + 1, :], (CH, channels))
        bt_ref[j] = row.astype(jnp.bfloat16)
    sums_ref[...] = jnp.zeros_like(sums_ref)

    def step(index, carry):
        hots = []
        crosses = []
        for k in range(JBLK):
            j = index * JBLK + k
            hots.append(hot_rows(bt_ref, j, channels))
            source = [
                jnp.concatenate([src_ref[j, p], src_ref[j, p]], axis=0) for p in range(3 * windows)
            ]
            for g in range(owners):
                receiver = [rec_ref[p, pl.ds(g * CH, CH)] for p in range(3 * windows)]
                crosses.append(cross_piece(source, receiver, windows))
        hot = jnp.concatenate(hots, axis=1)
        cross = jnp.concatenate(crosses, axis=0)
        sums_ref[...] += jnp.dot(hot, cross, preferred_element_type=jnp.float32)
        return carry

    lax.fori_loop(0, SOURCES // JBLK, step, 0)
    sums = sums_ref[...]
    high = sums.astype(jnp.bfloat16)
    low = (sums - high.astype(jnp.float32)).astype(jnp.bfloat16)
    table = table_ref[...]
    lags = jnp.dot(high, table, preferred_element_type=jnp.float32)
    lags = lags + jnp.dot(low, table, preferred_element_type=jnp.float32)
    out_ref[...] = lags.astype(jnp.bfloat16)


def bin_sums(plan, gathered, table, windows):
    owners, rows, _ = gathered.shape
    channels = owners * CH
    vmem = pl.BlockSpec(memory_space=pltpu.VMEM)
    return pl.pallas_call(
        functools.partial(bin_kernel, windows),
        in_specs=[pl.BlockSpec(memory_space=pltpu.SMEM), vmem, vmem],
        out_specs=vmem,
        out_shape=jax.ShapeDtypeStruct((NBINS, LAGS), jnp.bfloat16),
        scratch_shapes=[
            pltpu.VMEM((3 * windows, channels, BAND), jnp.float32),
            pltpu.VMEM((SOURCES, 3 * windows, 8, BAND), jnp.float32),
            pltpu.VMEM((SOURCES, CH, channels), jnp.bfloat16),
            pltpu.VMEM((NBINS, 2 * BAND), jnp.float32),
        ],
        compiler_params=pltpu.CompilerParams(vmem_limit_bytes=40 * 1024 * 1024),
    )(plan, gathered, table)


def lag_table(offset, span_bins, lag_count, bin_total):
    numbers = offset + 1 + lax.iota(jnp.int32, span_bins)
    shifts = lax.iota(jnp.int32, lag_count) - lag_count // 2
    phase = jnp.mod(numbers[:, None] * shifts[None, :], 2 * bin_total)
    angle = phase.astype(jnp.float32) * (math.pi / bin_total)
    factor = 1.0 / math.sqrt(bin_total)
    table = (jnp.stack([jnp.cos(angle), -jnp.sin(angle)]) * factor).astype(jnp.bfloat16)
    return table.reshape(2 * span_bins, lag_count)


def per_device(spectra, plan, pair_bins):
    windows = spectra.shape[0]
    freq = spectra.shape[3]
    owners = lax.axis_size("chan")
    win_size = lax.axis_size("win")
    own = lax.axis_index("chan")
    outgoing = whiten(spectra, pair_bins.reshape(CH, SOURCES))
    gathered = lax.all_to_all(outgoing, "chan", split_axis=0, concat_axis=0, tiled=True)
    table = lag_table(own * BAND, BAND, LAGS, freq)
    partial = bin_sums(plan, gathered, table, windows)
    bin_block = NBINS // owners
    arrived = lax.all_to_all(
        partial.reshape(owners, bin_block, LAGS), "chan", split_axis=0, concat_axis=0, tiled=True
    )
    total = jnp.sum(arrived.astype(jnp.float32), axis=0)
    named = gathered[:, 2 * windows * CH:, :SOURCES].astype(jnp.float32)
    mine = (own * bin_block + lax.iota(jnp.int32, bin_block)).astype(jnp.float32)
    counts = jnp.sum((named[None] == mine[:, None, None, None]).astype(jnp.float32), axis=(1, 2, 3))
    summed = total
    for d in range(1, win_size):
        summed = summed + lax.ppermute(
            total, "win", [(i, (i + d) % win_size) for i in range(win_size)]
        )
    return summed / jnp.sqrt(counts * (windows * win_size))[:, None]


def solution(mesh):
    placed = (P("win", None, "chan", None), P(), P("chan", None, None))
    return jax.shard_map(
        per_device, mesh=mesh, in_specs=placed, out_specs=P("chan", None), check_vma=False
    )
```

```python
import functools
import math

import jax
import jax.numpy as jnp
from jax import lax
from jax.experimental import pallas as pl
from jax.experimental.pallas import tpu as pltpu
from jax.sharding import PartitionSpec as P

LAGS = 512
BAND = 128
STEPS = 4
NBINS = 256
CH = 16
HALF = CH // 2
SOURCES = STEPS * CH
JBLK = 32


def whiten_kernel(spectra_ref, bins_ref, out_ref):
    chunks = out_ref.shape[0]
    windows = spectra_ref.shape[0]
    bins = bins_ref[...].astype(jnp.float32)
    bins = jnp.concatenate([bins[:HALF], bins[HALF:]], axis=1).astype(jnp.bfloat16)
    for c in range(chunks):
        lanes = pl.ds(c * BAND, BAND)
        for w in range(windows):
            real = spectra_ref[w, 0, :, lanes]
            imaginary = spectra_ref[w, 1, :, lanes]
            energy = real * real + imaginary * imaginary
            level = jnp.sqrt(jnp.mean(energy, axis=1, keepdims=True) + 1e-06)
            inverse = 1.0 / level
            out_ref[c, pl.ds(2 * w * CH, CH), :] = (real * inverse).astype(jnp.bfloat16)
            out_ref[c, pl.ds((2 * w + 1) * CH, CH), :] = (imaginary * inverse).astype(jnp.bfloat16)
        out_ref[c, pl.ds(2 * windows * CH, HALF), :] = bins


def whiten(spectra, bins):
    windows, _, channels, freq = spectra.shape
    owners = freq // BAND
    rows = 2 * windows * CH + HALF
    step = 16
    return pl.pallas_call(
        whiten_kernel,
        grid=(owners // step,),
        in_specs=[
            pl.BlockSpec((windows, 2, channels, step * BAND), lambda i: (0, 0, 0, i)),
            pl.BlockSpec(bins.shape, lambda i: (0, 0)),
        ],
        out_specs=pl.BlockSpec((step, rows, BAND), lambda i: (i, 0, 0)),
        out_shape=pltpu.VMEM((owners, rows, BAND), jnp.bfloat16),
    )(spectra, bins)


def hot_rows(bt_ref, j, channels):
    numbers = lax.broadcasted_iota(jnp.int32, (NBINS, channels), 0).astype(jnp.float32)
    named = jnp.broadcast_to(bt_ref[j][None], (NBINS // CH, CH, channels))
    same = numbers.astype(jnp.bfloat16) == named.reshape(NBINS, channels)
    return jnp.where(same, jnp.ones((), jnp.bfloat16), jnp.zeros((), jnp.bfloat16))


def cross_piece(source, receiver, windows):
    first = second = third = None
    for w in range(windows):
        products = [source[3 * w + p] * receiver[3 * w + p] for p in range(3)]
        if first is None:
            first, second, third = products
        else:
            first = first + products[0]
            second = second + products[1]
            third = third + products[2]
    real = (first - third).astype(jnp.bfloat16)
    imaginary = (first + second).astype(jnp.bfloat16)
    return jnp.concatenate([real, imaginary], axis=1)


def bin_kernel(windows, plan_ref, x_ref, table_ref, out_ref, rec_ref, src_ref, bt_ref, sums_ref):
    owners = x_ref.shape[0]
    channels = owners * CH
    for w in range(windows):
        real_slabs = x_ref[:, pl.ds(2 * w * CH, CH), :].astype(jnp.float32)
        imaginary_slabs = x_ref[:, pl.ds((2 * w + 1) * CH, CH), :].astype(jnp.float32)
        for h in range(2):
            rows = pl.ds(h * owners * HALF, owners * HALF)
            real = real_slabs[:, h * HALF:(h + 1) * HALF].reshape(owners * HALF, BAND)
            imaginary = imaginary_slabs[:, h * HALF:(h + 1) * HALF].reshape(owners * HALF, BAND)
            rec_ref[3 * w, rows] = real
            rec_ref[3 * w + 1, rows] = -(real + imaginary)
            rec_ref[3 * w + 2, rows] = real - imaginary
    for q in range(STEPS):
        for w in range(windows):
            real = x_ref[plan_ref[q], pl.ds(2 * w * CH, CH), :].astype(jnp.float32)
            imaginary = x_ref[plan_ref[q], pl.ds((2 * w + 1) * CH, CH), :].astype(jnp.float32)
            for p, value in enumerate((real + imaginary, real, imaginary)):
                for j in range(CH):
                    row = jnp.broadcast_to(value[j:j + 1, :], (8, BAND))
                    src_ref[q * CH + j, 3 * w + p] = row
    bins = x_ref[:, pl.ds(2 * windows * CH, HALF), :].astype(jnp.float32)
    turned = bins.reshape(owners * HALF, BAND).T
    for j in range(SOURCES):
        row = jnp.concatenate([turned[j:j + 1], turned[SOURCES + j:SOURCES + j + 1]], axis=1)
        bt_ref[j] = jnp.broadcast_to(row, (CH, channels)).astype(jnp.bfloat16)
    sums_ref[...] = jnp.zeros_like(sums_ref)

    def step(index, carry):
        hots = []
        crosses = []
        for k in range(JBLK):
            j = index * JBLK + k
            hots.append(hot_rows(bt_ref, j, channels))
            source = [
                jnp.concatenate([src_ref[j, p], src_ref[j, p]], axis=0) for p in range(3 * windows)
            ]
            for g in range(owners):
                receiver = [rec_ref[p, pl.ds(g * CH, CH)] for p in range(3 * windows)]
                crosses.append(cross_piece(source, receiver, windows))
        hot = jnp.concatenate(hots, axis=1)
        cross = jnp.concatenate(crosses, axis=0)
        sums_ref[...] += jnp.dot(hot, cross, preferred_element_type=jnp.float32)
        return carry

    lax.fori_loop(0, SOURCES // JBLK, step, 0)
    sums = sums_ref[...]
    high = sums.astype(jnp.bfloat16)
    low = (sums - high.astype(jnp.float32)).astype(jnp.bfloat16)
    table = table_ref[...]
    lags = jnp.dot(high, table, preferred_element_type=jnp.float32)
    lags = lags + jnp.dot(low, table, preferred_element_type=jnp.float32)
    out_ref[...] = lags.astype(jnp.bfloat16)


def bin_sums(plan, gathered, table, windows):
    owners, rows, _ = gathered.shape
    channels = owners * CH
    vmem = pl.BlockSpec(memory_space=pltpu.VMEM)
    return pl.pallas_call(
        functools.partial(bin_kernel, windows),
        in_specs=[pl.BlockSpec(memory_space=pltpu.SMEM), vmem, vmem],
        out_specs=vmem,
        out_shape=pltpu.VMEM((NBINS, LAGS), jnp.bfloat16),
        scratch_shapes=[
            pltpu.VMEM((3 * windows, channels, BAND), jnp.float32),
            pltpu.VMEM((SOURCES, 3 * windows, 8, BAND), jnp.float32),
            pltpu.VMEM((SOURCES, CH, channels), jnp.bfloat16),
            pltpu.VMEM((NBINS, 2 * BAND), jnp.float32),
        ],
        compiler_params=pltpu.CompilerParams(vmem_limit_bytes=40 * 1024 * 1024),
    )(plan, gathered, table)


def lag_table(offset, span_bins, lag_count, bin_total):
    numbers = offset + 1 + lax.iota(jnp.int32, span_bins)
    shifts = lax.iota(jnp.int32, lag_count) - lag_count // 2
    phase = jnp.mod(numbers[:, None] * shifts[None, :], 2 * bin_total)
    angle = phase.astype(jnp.float32) * (math.pi / bin_total)
    factor = 1.0 / math.sqrt(bin_total)
    table = (jnp.stack([jnp.cos(angle), -jnp.sin(angle)]) * factor).astype(jnp.bfloat16)
    return table.reshape(2 * span_bins, lag_count)


def per_device(spectra, plan, pair_bins):
    windows = spectra.shape[0]
    freq = spectra.shape[3]
    owners = lax.axis_size("chan")
    win_size = lax.axis_size("win")
    own = lax.axis_index("chan")
    outgoing = whiten(spectra, pair_bins.reshape(CH, SOURCES))
    gathered = lax.all_to_all(outgoing, "chan", split_axis=0, concat_axis=0, tiled=True)
    table = lag_table(own * BAND, BAND, LAGS, freq)
    partial = bin_sums(plan, gathered, table, windows)
    bin_block = NBINS // owners
    arrived = lax.all_to_all(
        partial.reshape(owners, bin_block, LAGS), "chan", split_axis=0, concat_axis=0, tiled=True
    )
    total = jnp.sum(arrived.astype(jnp.float32), axis=0)
    named = gathered[:, 2 * windows * CH:].astype(jnp.float32)
    mine = (own * bin_block + lax.iota(jnp.int32, bin_block)).astype(jnp.float32)
    counts = jnp.sum((named[None] == mine[:, None, None, None]).astype(jnp.float32), axis=(1, 2, 3))
    summed = total
    for d in range(1, win_size):
        summed = summed + lax.ppermute(
            total, "win", [(i, (i + d) % win_size) for i in range(win_size)]
        )
    return summed / jnp.sqrt(counts * (windows * win_size))[:, None]


def solution(mesh):
    placed = (P("win", None, "chan", None), P(), P("chan", None, None))
    return jax.shard_map(
        per_device, mesh=mesh, in_specs=placed, out_specs=P("chan", None), check_vma=False
    )
```

```python
import functools
import math

import jax
import jax.numpy as jnp
from jax import lax
from jax.experimental import pallas as pl
from jax.experimental.pallas import tpu as pltpu
from jax.sharding import PartitionSpec as P

LAGS = 512
BAND = 128
STEPS = 4
NBINS = 256
CH = 16
HALF = CH // 2
SOURCES = STEPS * CH
JBLK = 32


def whiten_kernel(spectra_ref, bins_ref, out_ref):
    chunks = out_ref.shape[0]
    windows = spectra_ref.shape[0]
    bins = bins_ref[...].astype(jnp.float32)
    bins = jnp.concatenate([bins[:HALF], bins[HALF:]], axis=1).astype(jnp.bfloat16)
    for c in range(chunks):
        lanes = pl.ds(c * BAND, BAND)
        for w in range(windows):
            real = spectra_ref[w, 0, :, lanes]
            imaginary = spectra_ref[w, 1, :, lanes]
            energy = real * real + imaginary * imaginary
            inverse = lax.rsqrt(jnp.mean(energy, axis=1, keepdims=True) + 1e-06)
            out_ref[c, pl.ds(2 * w * CH, CH), :] = (real * inverse).astype(jnp.bfloat16)
            out_ref[c, pl.ds((2 * w + 1) * CH, CH), :] = (imaginary * inverse).astype(jnp.bfloat16)
        out_ref[c, pl.ds(2 * windows * CH, HALF), :] = bins


def whiten(spectra, bins):
    windows, _, channels, freq = spectra.shape
    owners = freq // BAND
    rows = 2 * windows * CH + HALF
    step = 16
    return pl.pallas_call(
        whiten_kernel,
        grid=(owners // step,),
        in_specs=[
            pl.BlockSpec((windows, 2, channels, step * BAND), lambda i: (0, 0, 0, i)),
            pl.BlockSpec(bins.shape, lambda i: (0, 0)),
        ],
        out_specs=pl.BlockSpec((step, rows, BAND), lambda i: (i, 0, 0)),
        out_shape=pltpu.VMEM((owners, rows, BAND), jnp.bfloat16),
    )(spectra, bins)


def hot_rows(bt_ref, j, channels):
    numbers = lax.broadcasted_iota(jnp.int32, (NBINS, channels), 0).astype(jnp.float32)
    named = jnp.broadcast_to(bt_ref[j][None], (NBINS // CH, CH, channels))
    same = numbers.astype(jnp.bfloat16) == named.reshape(NBINS, channels)
    return jnp.where(same, jnp.ones((), jnp.bfloat16), jnp.zeros((), jnp.bfloat16))


def cross_piece(source, receiver, windows):
    first = second = third = None
    for w in range(windows):
        products = [source[3 * w + p] * receiver[3 * w + p] for p in range(3)]
        if first is None:
            first, second, third = products
        else:
            first = first + products[0]
            second = second + products[1]
            third = third + products[2]
    real = (first - third).astype(jnp.bfloat16)
    imaginary = (first + second).astype(jnp.bfloat16)
    return jnp.concatenate([real, imaginary], axis=1)


def bin_kernel(windows, plan_ref, x_ref, table_ref, out_ref, rec_ref, src_ref, bt_ref, sums_ref):
    owners = x_ref.shape[0]
    channels = owners * CH
    for w in range(windows):
        real_slabs = x_ref[:, pl.ds(2 * w * CH, CH), :].astype(jnp.float32)
        imaginary_slabs = x_ref[:, pl.ds((2 * w + 1) * CH, CH), :].astype(jnp.float32)
        for h in range(2):
            rows = pl.ds(h * owners * HALF, owners * HALF)
            real = real_slabs[:, h * HALF:(h + 1) * HALF].reshape(owners * HALF, BAND)
            imaginary = imaginary_slabs[:, h * HALF:(h + 1) * HALF].reshape(owners * HALF, BAND)
            rec_ref[3 * w, rows] = real
            rec_ref[3 * w + 1, rows] = -(real + imaginary)
            rec_ref[3 * w + 2, rows] = real - imaginary
    for q in range(STEPS):
        for w in range(windows):
            real = x_ref[plan_ref[q], pl.ds(2 * w * CH, CH), :].astype(jnp.float32)
            imaginary = x_ref[plan_ref[q], pl.ds((2 * w + 1) * CH, CH), :].astype(jnp.float32)
            for p, value in enumerate((real + imaginary, real, imaginary)):
                for j in range(CH):
                    row = jnp.broadcast_to(value[j:j + 1, :], (8, BAND))
                    src_ref[q * CH + j, 3 * w + p] = row
    bins = x_ref[:, pl.ds(2 * windows * CH, HALF), :].astype(jnp.float32)
    turned = bins.reshape(owners * HALF, BAND).T
    for j in range(SOURCES):
        row = jnp.concatenate([turned[j:j + 1], turned[SOURCES + j:SOURCES + j + 1]], axis=1)
        bt_ref[j] = jnp.broadcast_to(row, (CH, channels)).astype(jnp.bfloat16)
    sums_ref[...] = jnp.zeros_like(sums_ref)

    def step(index, carry):
        hots = []
        crosses = []
        for k in range(JBLK):
            j = index * JBLK + k
            hots.append(hot_rows(bt_ref, j, channels))
            source = [
                jnp.concatenate([src_ref[j, p], src_ref[j, p]], axis=0) for p in range(3 * windows)
            ]
            for g in range(owners):
                receiver = [rec_ref[p, pl.ds(g * CH, CH)] for p in range(3 * windows)]
                crosses.append(cross_piece(source, receiver, windows))
        hot = jnp.concatenate(hots, axis=1)
        cross = jnp.concatenate(crosses, axis=0)
        sums_ref[...] += jnp.dot(hot, cross, preferred_element_type=jnp.float32)
        return carry

    lax.fori_loop(0, SOURCES // JBLK, step, 0)
    sums = sums_ref[...]
    high = sums.astype(jnp.bfloat16)
    low = (sums - high.astype(jnp.float32)).astype(jnp.bfloat16)
    table = table_ref[...]
    both = jnp.concatenate([high, low], axis=1)
    lags = jnp.dot(
        both, jnp.concatenate([table, table], axis=0), preferred_element_type=jnp.float32
    )
    out_ref[...] = lags.astype(jnp.bfloat16)


def bin_sums(plan, gathered, table, windows):
    owners, rows, _ = gathered.shape
    channels = owners * CH
    vmem = pl.BlockSpec(memory_space=pltpu.VMEM)
    return pl.pallas_call(
        functools.partial(bin_kernel, windows),
        in_specs=[pl.BlockSpec(memory_space=pltpu.SMEM), vmem, vmem],
        out_specs=vmem,
        out_shape=pltpu.VMEM((NBINS, LAGS), jnp.bfloat16),
        scratch_shapes=[
            pltpu.VMEM((3 * windows, channels, BAND), jnp.float32),
            pltpu.VMEM((SOURCES, 3 * windows, 8, BAND), jnp.float32),
            pltpu.VMEM((SOURCES, CH, channels), jnp.bfloat16),
            pltpu.VMEM((NBINS, 2 * BAND), jnp.float32),
        ],
        compiler_params=pltpu.CompilerParams(vmem_limit_bytes=40 * 1024 * 1024),
    )(plan, gathered, table)


def lag_table(offset, span_bins, lag_count, bin_total):
    numbers = offset + 1 + lax.iota(jnp.int32, span_bins)
    shifts = lax.iota(jnp.int32, lag_count) - lag_count // 2
    phase = jnp.mod(numbers[:, None] * shifts[None, :], 2 * bin_total)
    angle = phase.astype(jnp.float32) * (math.pi / bin_total)
    factor = 1.0 / math.sqrt(bin_total)
    table = (jnp.stack([jnp.cos(angle), -jnp.sin(angle)]) * factor).astype(jnp.bfloat16)
    return table.reshape(2 * span_bins, lag_count)


def per_device(spectra, plan, pair_bins):
    windows = spectra.shape[0]
    freq = spectra.shape[3]
    owners = lax.axis_size("chan")
    win_size = lax.axis_size("win")
    own = lax.axis_index("chan")
    outgoing = whiten(spectra, pair_bins.reshape(CH, SOURCES))
    gathered = lax.all_to_all(outgoing, "chan", split_axis=0, concat_axis=0, tiled=True)
    table = lag_table(own * BAND, BAND, LAGS, freq)
    partial = bin_sums(plan, gathered, table, windows)
    bin_block = NBINS // owners
    arrived = lax.all_to_all(
        partial.reshape(owners, bin_block, LAGS), "chan", split_axis=0, concat_axis=0, tiled=True
    )
    total = jnp.sum(arrived.astype(jnp.float32), axis=0)
    named = gathered[:, 2 * windows * CH:].astype(jnp.float32)
    mine = (own * bin_block + lax.iota(jnp.int32, bin_block)).astype(jnp.float32)
    counts = jnp.sum((named[None] == mine[:, None, None, None]).astype(jnp.float32), axis=(1, 2, 3))
    scale = 1.0 / jnp.sqrt(counts * (windows * win_size))
    scaled = total * scale[:, None]
    sent = scaled
    summed = scaled
    for d in range(1, win_size):
        passed = lax.ppermute(sent, "win", [(i, (i + d) % win_size) for i in range(win_size)])
        summed = summed + passed
    return summed


def solution(mesh):
    placed = (P("win", None, "chan", None), P(), P("chan", None, None))
    return jax.shard_map(
        per_device, mesh=mesh, in_specs=placed, out_specs=P("chan", None), check_vma=False
    )
```

```python
import functools
import math

import jax
import jax.numpy as jnp
from jax import lax
from jax.experimental import pallas as pl
from jax.experimental.pallas import tpu as pltpu
from jax.sharding import PartitionSpec as P

LAGS = 512
BAND = 128
STEPS = 4
NBINS = 256
CH = 16
HALF = CH // 2
SOURCES = STEPS * CH
JBLK = 32


def whiten_kernel(spectra_ref, bins_ref, out_ref):
    chunks = out_ref.shape[0]
    windows = spectra_ref.shape[0]
    bins = bins_ref[...].astype(jnp.float32)
    bins = jnp.concatenate([bins[:HALF], bins[HALF:]], axis=1).astype(jnp.bfloat16)
    for c in range(chunks):
        lanes = pl.ds(c * BAND, BAND)
        for w in range(windows):
            real = spectra_ref[w, 0, :, lanes]
            imaginary = spectra_ref[w, 1, :, lanes]
            energy = real * real + imaginary * imaginary
            level = jnp.sqrt(jnp.mean(energy, axis=1, keepdims=True) + 1e-06)
            inverse = 1.0 / level
            out_ref[c, pl.ds(2 * w * CH, CH), :] = (real * inverse).astype(jnp.bfloat16)
            out_ref[c, pl.ds((2 * w + 1) * CH, CH), :] = (imaginary * inverse).astype(jnp.bfloat16)
        out_ref[c, pl.ds(2 * windows * CH, HALF), :] = bins


def whiten(spectra, bins):
    windows, _, channels, freq = spectra.shape
    owners = freq // BAND
    rows = 2 * windows * CH + HALF
    step = 16
    return pl.pallas_call(
        whiten_kernel,
        grid=(owners // step,),
        in_specs=[
            pl.BlockSpec((windows, 2, channels, step * BAND), lambda i: (0, 0, 0, i)),
            pl.BlockSpec(bins.shape, lambda i: (0, 0)),
        ],
        out_specs=pl.BlockSpec((step, rows, BAND), lambda i: (i, 0, 0)),
        out_shape=pltpu.VMEM((owners, rows, BAND), jnp.bfloat16),
    )(spectra, bins)


def hot_rows(bt_ref, j, channels):
    numbers = lax.broadcasted_iota(jnp.int32, (NBINS, channels), 0).astype(jnp.float32)
    named = jnp.broadcast_to(bt_ref[j][None], (NBINS // CH, CH, channels))
    same = numbers.astype(jnp.bfloat16) == named.reshape(NBINS, channels)
    return jnp.where(same, jnp.ones((), jnp.bfloat16), jnp.zeros((), jnp.bfloat16))


def cross_piece(source, receiver, windows):
    first = second = third = None
    for w in range(windows):
        products = [source[3 * w + p] * receiver[3 * w + p] for p in range(3)]
        if first is None:
            first, second, third = products
        else:
            first = first + products[0]
            second = second + products[1]
            third = third + products[2]
    real = (first - third).astype(jnp.bfloat16)
    imaginary = (first + second).astype(jnp.bfloat16)
    return jnp.concatenate([real, imaginary], axis=1)


def bin_kernel(windows, plan_ref, x_ref, table_ref, out_ref, rec_ref, src_ref, bt_ref, sums_ref):
    owners = x_ref.shape[0]
    channels = owners * CH
    for w in range(windows):
        real_slabs = x_ref[:, pl.ds(2 * w * CH, CH), :].astype(jnp.float32)
        imaginary_slabs = x_ref[:, pl.ds((2 * w + 1) * CH, CH), :].astype(jnp.float32)
        for h in range(2):
            rows = pl.ds(h * owners * HALF, owners * HALF)
            real = real_slabs[:, h * HALF:(h + 1) * HALF].reshape(owners * HALF, BAND)
            imaginary = imaginary_slabs[:, h * HALF:(h + 1) * HALF].reshape(owners * HALF, BAND)
            rec_ref[3 * w, rows] = real
            rec_ref[3 * w + 1, rows] = -(real + imaginary)
            rec_ref[3 * w + 2, rows] = real - imaginary
    for q in range(STEPS):
        for w in range(windows):
            real = x_ref[plan_ref[q], pl.ds(2 * w * CH, CH), :].astype(jnp.float32)
            imaginary = x_ref[plan_ref[q], pl.ds((2 * w + 1) * CH, CH), :].astype(jnp.float32)
            for p, value in enumerate((real + imaginary, real, imaginary)):
                for j in range(CH):
                    row = jnp.broadcast_to(value[j:j + 1, :], (8, BAND))
                    src_ref[q * CH + j, 3 * w + p] = row
    bins = x_ref[:, pl.ds(2 * windows * CH, HALF), :].astype(jnp.float32)
    turned = bins.reshape(owners * HALF, BAND).T
    for j in range(SOURCES):
        row = jnp.concatenate([turned[j:j + 1], turned[SOURCES + j:SOURCES + j + 1]], axis=1)
        bt_ref[j] = jnp.broadcast_to(row, (CH, channels)).astype(jnp.bfloat16)
    sums_ref[...] = jnp.zeros_like(sums_ref)

    def step(index, carry):
        hots = []
        crosses = []
        for k in range(JBLK):
            j = index * JBLK + k
            hots.append(hot_rows(bt_ref, j, channels))
            source = [
                jnp.concatenate([src_ref[j, p], src_ref[j, p]], axis=0) for p in range(3 * windows)
            ]
            for g in range(owners):
                receiver = [rec_ref[p, pl.ds(g * CH, CH)] for p in range(3 * windows)]
                crosses.append(cross_piece(source, receiver, windows))
        hot = jnp.concatenate(hots, axis=1)
        cross = jnp.concatenate(crosses, axis=0)
        sums_ref[...] += jnp.dot(hot, cross, preferred_element_type=jnp.float32)
        return carry

    lax.fori_loop(0, SOURCES // JBLK, step, 0)
    sums = sums_ref[...]
    high = sums.astype(jnp.bfloat16)
    low = (sums - high.astype(jnp.float32)).astype(jnp.bfloat16)
    table = table_ref[...]
    both = jnp.concatenate([high, low], axis=1)
    tables = jnp.concatenate([table, table], axis=0)
    lags = jnp.dot(both, tables, preferred_element_type=jnp.float32)
    out_ref[...] = lags.astype(jnp.bfloat16)


def bin_sums(plan, gathered, table, windows):
    owners, rows, _ = gathered.shape
    channels = owners * CH
    vmem = pl.BlockSpec(memory_space=pltpu.VMEM)
    return pl.pallas_call(
        functools.partial(bin_kernel, windows),
        in_specs=[pl.BlockSpec(memory_space=pltpu.SMEM), vmem, vmem],
        out_specs=vmem,
        out_shape=pltpu.VMEM((NBINS, LAGS), jnp.bfloat16),
        scratch_shapes=[
            pltpu.VMEM((3 * windows, channels, BAND), jnp.float32),
            pltpu.VMEM((SOURCES, 3 * windows, 8, BAND), jnp.float32),
            pltpu.VMEM((SOURCES, CH, channels), jnp.bfloat16),
            pltpu.VMEM((NBINS, 2 * BAND), jnp.float32),
        ],
        compiler_params=pltpu.CompilerParams(vmem_limit_bytes=40 * 1024 * 1024),
    )(plan, gathered, table)


def lag_table(offset, span_bins, lag_count, bin_total):
    numbers = offset + 1 + lax.iota(jnp.int32, span_bins)
    shifts = lax.iota(jnp.int32, lag_count) - lag_count // 2
    phase = jnp.mod(numbers[:, None] * shifts[None, :], 2 * bin_total)
    angle = phase.astype(jnp.float32) * (math.pi / bin_total)
    factor = 1.0 / math.sqrt(bin_total)
    table = (jnp.stack([jnp.cos(angle), -jnp.sin(angle)]) * factor).astype(jnp.bfloat16)
    return table.reshape(2 * span_bins, lag_count)


def per_device(spectra, plan, pair_bins):
    windows = spectra.shape[0]
    freq = spectra.shape[3]
    owners = lax.axis_size("chan")
    win_size = lax.axis_size("win")
    own = lax.axis_index("chan")
    outgoing = whiten(spectra, pair_bins.reshape(CH, SOURCES))
    gathered = lax.all_to_all(outgoing, "chan", split_axis=0, concat_axis=0, tiled=True)
    table = lag_table(own * BAND, BAND, LAGS, freq)
    partial = bin_sums(plan, gathered, table, windows)
    bin_block = NBINS // owners
    arrived = lax.all_to_all(
        partial.reshape(owners, bin_block, LAGS), "chan", split_axis=0, concat_axis=0, tiled=True
    )
    total = jnp.sum(arrived.astype(jnp.float32), axis=0)
    named = gathered[:, 2 * windows * CH:].astype(jnp.float32)
    mine = (own * bin_block + lax.iota(jnp.int32, bin_block)).astype(jnp.float32)
    counts = jnp.sum((named[None] == mine[:, None, None, None]).astype(jnp.float32), axis=(1, 2, 3))
    summed = total
    for d in range(1, win_size):
        summed = summed + lax.ppermute(
            total, "win", [(i, (i + d) % win_size) for i in range(win_size)]
        )
    return summed / jnp.sqrt(counts * (windows * win_size))[:, None]


def solution(mesh):
    placed = (P("win", None, "chan", None), P(), P("chan", None, None))
    return jax.shard_map(
        per_device, mesh=mesh, in_specs=placed, out_specs=P("chan", None), check_vma=False
    )
```
